32 devices in a mesh: groups: 2 (over x), tm: 16 (over z, y, core).
Axes of the slice: x: 2, y: 2, z: 4, core: 2. Of those that a mesh axis runs over, the one named last changes fastest.
Arguments:
- queries: bfloat16 [12288, 1280], P(('groups', 'tm')), parts along dimension 0, may hold values from -110 to 110
- key_rows: bfloat16 [12288, 1280], P(('groups', 'tm')), parts along dimension 0, may hold values from -6 to 6
- value_rows: bfloat16 [12288, 1280], P(('groups', 'tm')), parts along dimension 0, may hold values from -6 to 6
- out_grad: bfloat16 [12288, 1280], P(('groups', 'tm')), parts along dimension 0, may hold values from -6 to 6
- block_lists: int32 [96, 8], P(('groups', 'tm')), parts along dimension 0, may hold values from 0 to 47, as said below
- list_counts: int32 [96], P(('groups', 'tm')), parts along dimension 0, may hold values from 4 to 8, as said below
Outputs:
- attended: bfloat16 [12288, 1280], P(('groups', 'tm')), parts along dimension 0
- query_grad: bfloat16 [12288, 1280], P(('groups', 'tm')), parts along dimension 0
- key_grad: bfloat16 [12288, 1280], P(('groups', 'tm')), parts along dimension 0
- value_grad: bfloat16 [12288, 1280], P(('groups', 'tm')), parts along dimension 0
The draws below stay inside these ranges and needn't reach their ends.
There are 2 independent parts, one for each index of `groups`. The reference program is written for one: setup_inputs(seed, part) draws one part's arguments, and reference() takes and returns one part's arrays. A program takes and returns all parts, laid end to end along the dimension named above; each array names one. Nothing has to cross between parts.
Inputs may be any that keep to these rules, and one draw needn't show every extreme that they name: `block_lists`: the first list_counts[g] entries of row g are distinct blocks lying in the shards at most two away from the shard of block g (a shard holds 3 blocks); the other entries equal g. `list_counts`: how many leading entries of a row of block_lists count.
All inputs are finite; a program needn't handle non-finite values.
Results may differ from the reference program's by a relative error of at most 0.023.
Values may be sent and summed in bfloat16 or wider, within the bound.
No kernel may reach another device: no remote copies, remote signals or barrier semaphores. Data moves between devices by JAX's collectives and lax.ppermute only.
A program may use at most 192 MiB of HBM per device.

```python
import math
import jax
import jax.numpy as jnp
from jax import lax

HEADS = 20
HEAD_DIM = 64
D = 1280
BLK = 128
LIST = 8
NB = 3
NBLK = 48
SEQ = 6144


def attention_pair(key):
    key_source = jax.random.fold_in(key, 11)
    query_source = jax.random.fold_in(key, 12)
    key_base = jnp.clip(jax.random.normal(key_source, (SEQ, D), jnp.float32), -6.0, 6.0)
    query_base = jnp.clip(jax.random.normal(query_source, (SEQ, D), jnp.float32), -6.0, 6.0)
    return (query_base, key_base)


def draw_queries(key, part):
    return attention_pair(key)[0].astype(jnp.bfloat16)


def draw_key_rows(key, part):
    return attention_pair(key)[1].astype(jnp.bfloat16)


def block_structure(key):
    list_source = jax.random.fold_in(key, 21)
    subkeys = jax.random.split(list_source, 7)
    block_ids = jnp.arange(NBLK, dtype=jnp.int32)
    shard_ids = block_ids // NB
    far_low = jax.random.randint(subkeys[0], (NBLK,), 0, NB)
    far_high = jax.random.randint(subkeys[1], (NBLK,), 0, NB)
    near_low = jax.random.randint(subkeys[2], (NBLK,), 0, NB - 1)
    near_high = jax.random.randint(subkeys[3], (NBLK,), 1, NB)
    second_side = jax.random.randint(subkeys[4], (NBLK,), 0, 2)
    extra_on = jax.random.randint(subkeys[5], (NBLK,), 0, 2)
    extra_on = jnp.where(block_ids == NBLK // 2, 1, extra_on)
    second_step = jax.random.randint(subkeys[6], (NBLK,), 0, NB - 1)
    second = jnp.where(second_side == 0, (shard_ids - 2) * NB + (far_low + 1 + second_step) % NB, (shard_ids + 2) * NB + (far_high + 1 + second_step) % NB)
    candidates = jnp.stack([block_ids, block_ids - 1, block_ids + 1, (shard_ids - 2) * NB + far_low, (shard_ids + 2) * NB + far_high, (shard_ids - 1) * NB + near_low, (shard_ids + 1) * NB + near_high, second], axis=1).astype(jnp.int32)
    inside = (candidates >= 0) & (candidates < NBLK)
    inside = inside.at[:, 7].set(inside[:, 7] & (extra_on == 1))
    slot_ids = jnp.arange(LIST, dtype=jnp.int32)
    order_key = jnp.where(inside, 0, LIST).astype(jnp.int32) + slot_ids[None, :]
    order = jnp.argsort(order_key, axis=1, stable=True)
    ordered = jnp.take_along_axis(candidates, order, axis=1)
    counts = jnp.sum(inside.astype(jnp.int32), axis=1)
    lists = jnp.where(slot_ids[None, :] < counts[:, None], ordered, block_ids[:, None])
    return (lists.astype(jnp.int32), counts.astype(jnp.int32))


def draw_block_lists(key, part):
    return block_structure(key)[0]


def draw_list_counts(key, part):
    return block_structure(key)[1]


def block_scale(own_key, shape, cuts, least, high):
    level = 1.0
    for position, blocks in cuts:
        draws = jax.random.uniform(jax.random.fold_in(jax.random.fold_in(own_key, 6), position), (blocks,), jnp.float32, least / len(cuts), high / len(cuts))
        level = level * jnp.repeat(jnp.exp(draws), shape[position] // blocks).reshape((-1,) + (1,) * (len(shape) - 1 - position))
    return level


def centred(stream_key, shape, spread, bound, shards=(), held_as=jnp.bfloat16):
    factor_of = block_scale(stream_key, shape, shards, -0.22, 0.18) if shards else 1.0
    result = jax.random.normal(stream_key, shape, jnp.float32) * spread * factor_of
    return jnp.minimum(jnp.maximum(result, -bound), bound).astype(held_as)


def setup_inputs(seed: int = 0, part: int = 0) -> dict:
    keys = jax.random.split(jax.random.key(seed), 7)
    part_keys = jax.random.split(jax.random.fold_in(keys[6], part), 7)
    queries = draw_queries(jax.random.fold_in(jax.random.fold_in(keys[6], part), 71), part)
    key_rows = draw_key_rows(jax.random.fold_in(jax.random.fold_in(keys[6], part), 71), part)
    value_rows = centred(part_keys[2], (SEQ, D), 1.0, 6.0, ((0, 16),))
    out_grad = centred(part_keys[3], (SEQ, D), 1.0, 6.0, ((0, 16),))
    block_lists = draw_block_lists(jax.random.fold_in(jax.random.fold_in(keys[6], part), 71), part)
    list_counts = draw_list_counts(jax.random.fold_in(jax.random.fold_in(keys[6], part), 71), part)
    return {"queries": queries, "key_rows": key_rows, "value_rows": value_rows, "out_grad": out_grad, "block_lists": block_lists, "list_counts": list_counts}


def reference(queries, key_rows, value_rows, out_grad, block_lists, list_counts):
    tok_total, feature_width = queries.shape
    block_total = tok_total // BLK
    score_scale = 1.0 / math.sqrt(HEAD_DIM)
    query_blocks = queries.reshape(block_total, BLK, HEADS, HEAD_DIM)
    key_blocks = key_rows.reshape(block_total, BLK, HEADS, HEAD_DIM)
    value_blocks = value_rows.reshape(block_total, BLK, HEADS, HEAD_DIM)
    grad_blocks = out_grad.reshape(block_total, BLK, HEADS, HEAD_DIM)
    slot_ids = jnp.arange(LIST, dtype=jnp.int32)

    def visit(running, block_index):
        key_acc, value_acc = running
        listed = block_lists[block_index].astype(jnp.int32)
        live_keys = jnp.repeat(slot_ids < list_counts[block_index], BLK)
        key_sel = key_blocks[listed].reshape(LIST * BLK, HEADS, HEAD_DIM).astype(jnp.float32)
        value_sel = value_blocks[listed].reshape(LIST * BLK, HEADS, HEAD_DIM).astype(jnp.float32)
        query_here = query_blocks[block_index].astype(jnp.float32)
        grad_here = grad_blocks[block_index].astype(jnp.float32)
        scores = jnp.einsum('qhe,khe->hqk', query_here, key_sel) * score_scale
        scores = jnp.where(live_keys[None, None, :], scores, -jnp.inf)
        row_max = lax.optimization_barrier(jnp.max(scores, axis=-1, keepdims=True))
        raised = jnp.exp(scores - row_max)
        weights = raised / lax.optimization_barrier(jnp.sum(raised, axis=-1, keepdims=True))
        weights_low = lax.optimization_barrier(weights.astype(jnp.bfloat16))
        weights_wide = weights_low.astype(jnp.float32)
        attended = lax.optimization_barrier(jnp.einsum('hqk,khe->qhe', weights_wide, value_sel).astype(jnp.bfloat16))
        row_dot = lax.optimization_barrier(jnp.sum(grad_here * attended.astype(jnp.float32), axis=-1))
        weight_grad = jnp.einsum('qhe,khe->hqk', grad_here, value_sel)
        dscore = lax.optimization_barrier((weights * (weight_grad - jnp.transpose(row_dot)[:, :, None])).astype(jnp.bfloat16))
        dscore_wide = dscore.astype(jnp.float32)
        query_grad = (jnp.einsum('hqk,khe->qhe', dscore_wide, key_sel) * score_scale).astype(jnp.bfloat16)
        key_part = jnp.einsum('hqk,qhe->khe', dscore_wide, query_here) * score_scale
        value_part = jnp.einsum('hqk,qhe->khe', weights_wide, grad_here)
        key_acc = key_acc.at[listed].add(key_part.reshape(LIST, BLK, feature_width))
        value_acc = value_acc.at[listed].add(value_part.reshape(LIST, BLK, feature_width))
        return ((key_acc, value_acc), (attended.reshape(BLK, feature_width), query_grad.reshape(BLK, feature_width)))
    cleared = jnp.zeros((block_total, BLK, feature_width), jnp.float32)
    (key_acc, value_acc), (attended, query_grad) = lax.scan(visit, (cleared, cleared), jnp.arange(block_total, dtype=jnp.int32))
    return (attended.reshape(tok_total, feature_width), query_grad.reshape(tok_total, feature_width), key_acc.reshape(tok_total, feature_width).astype(jnp.bfloat16), value_acc.reshape(tok_total, feature_width).astype(jnp.bfloat16))
```

```python
import functools
import math

import jax
import jax.numpy as jnp
from jax import lax
from jax.experimental import pallas as pl
from jax.experimental.pallas import tpu as pltpu
from jax.sharding import PartitionSpec as P

HEADS = 20
HEAD_DIM = 64
WIDE = 2 * HEAD_DIM
BLK = 128
LIST = 8
MIN_LIVE = 4
QUAD = 4
PIECES = 2 * QUAD
CHUNKS = (1, 2, 2)
LOG2E = math.log2(math.e)
VMEM_LIMIT = 48 * 1024 * 1024


def swapped(x):
    return jnp.concatenate([x[:, HEAD_DIM:], x[:, :HEAD_DIM]], axis=1)


def pack_body(place, query_ref, grad_ref, key_ref, value_ref, *outs):
    side, core = place[0] // 2, place[0] % 2
    rows = query_ref.shape[0]
    left = lax.broadcasted_iota(jnp.int32, (rows, WIDE), 1) < HEAD_DIM
    for (first_ref, second_ref), pieces in (
        ((query_ref, grad_ref), outs[:QUAD]),
        ((key_ref, value_ref), outs[QUAD:]),
    ):
        for other in range(2):
            column = pl.ds(pl.multiple_of((side ^ other) * WIDE, WIDE), WIDE)
            first, second = first_ref[:, column], second_ref[:, column]
            low = jnp.where(left, first, swapped(second))
            high = jnp.where(left, swapped(first), second)
            pieces[2 * other][0] = jnp.where(core == 0, low, high)
            pieces[2 * other + 1][0] = jnp.where(core == 0, high, low)


def pack(place, queries, out_grad, key_rows, value_rows, start, heads):
    rows = queries.shape[0]
    source = pl.BlockSpec((rows, 2 * WIDE), lambda h, _: (0, start + h))
    piece = pl.BlockSpec((1, rows, WIDE), lambda h, _: (h, 0, 0))
    shape = jax.ShapeDtypeStruct((heads, rows, WIDE), jnp.bfloat16)
    outs = pl.pallas_call(
        pack_body,
        grid_spec=pltpu.PrefetchScalarGridSpec(
            num_scalar_prefetch=1,
            grid=(heads,),
            in_specs=[source] * 4,
            out_specs=[piece] * (2 * QUAD),
        ),
        out_shape=[shape] * (2 * QUAD),
        compiler_params=pltpu.CompilerParams(vmem_limit_bytes=VMEM_LIMIT),
        cost_estimate=pl.CostEstimate(
            flops=0, bytes_accessed=heads * rows * WIDE * 32, transcendentals=0
        ),
        name="pack",
    )(place, queries, out_grad, key_rows, value_rows)
    return outs[:QUAD], outs[QUAD:]


def unpack_body(place, *refs):
    query_parts, key_parts, outs = refs[:QUAD], refs[QUAD : 2 * QUAD], refs[-4:]
    side, core = place[0] // 2, place[0] % 2
    rows = query_parts[0].shape[1]
    left = lax.broadcasted_iota(jnp.int32, (rows, WIDE), 1) < HEAD_DIM
    for parts, (first_out, second_out) in ((query_parts, outs[:2]), (key_parts, outs[2:])):
        for other in range(2):
            column = pl.ds(pl.multiple_of((side ^ other) * WIDE, WIDE), WIDE)
            even, odd = parts[2 * other][0], parts[2 * other + 1][0]
            low = jnp.where(core == 0, even, odd)
            high = jnp.where(core == 0, odd, even)
            first_out[:, column] = jnp.where(left, low, swapped(high))
            second_out[:, column] = jnp.where(left, swapped(low), high)


def unpack(place, query_parts, key_parts, so_far, start, full_width):
    heads, rows, _ = query_parts[0].shape
    piece = pl.BlockSpec((1, rows, WIDE), lambda h, _: (h, 0, 0))
    target = pl.BlockSpec((rows, 2 * WIDE), lambda h, _: (0, start + h))
    kept = [] if so_far is None else list(so_far)
    return pl.pallas_call(
        unpack_body,
        grid_spec=pltpu.PrefetchScalarGridSpec(
            num_scalar_prefetch=1,
            grid=(heads,),
            in_specs=[piece] * (2 * QUAD) + [pl.BlockSpec(memory_space=pl.ANY)] * len(kept),
            out_specs=[target] * 4,
        ),
        out_shape=[jax.ShapeDtypeStruct((rows, full_width), jnp.bfloat16)] * 4,
        input_output_aliases={1 + 2 * QUAD + n: n for n in range(len(kept))},
        compiler_params=pltpu.CompilerParams(vmem_limit_bytes=VMEM_LIMIT),
        cost_estimate=pl.CostEstimate(
            flops=0, bytes_accessed=heads * rows * WIDE * 32, transcendentals=0
        ),
        name="unpack",
    )(place, *query_parts, *key_parts, *kept)


def attend_body(lists, counts, *refs, blocks):
    query_parts, key_parts = refs[:QUAD], refs[QUAD : QUAD + PIECES]
    results = refs[QUAD + PIECES : 2 * QUAD + PIECES]
    own = refs[2 * QUAD + PIECES : 3 * QUAD + PIECES]
    near, far, window, window_t, total, pair = refs[3 * QUAD + PIECES :]
    score_scale = 1.0 / math.sqrt(HEAD_DIM)
    exponent_scale = LOG2E * score_scale
    for piece in range(PIECES):
        for block in range(blocks):
            rows = key_parts[piece][0, block * BLK : (block + 1) * BLK, :]
            window[piece * blocks + block] = rows
            window_t[piece * blocks + block] = rows.T
    total[...] = jnp.zeros_like(total)
    left = lax.broadcasted_iota(jnp.int32, (BLK, WIDE), 1) < HEAD_DIM

    for piece in range(QUAD):

        def query_block(block, carry, piece=piece):
            rows = pl.ds(pl.multiple_of(block * BLK, BLK), BLK)
            query_grad = query_parts[piece][0, rows, :]
            nothing = jnp.zeros_like(query_grad)
            operand = jnp.concatenate(
                [jnp.where(left, query_grad, nothing), jnp.where(left, nothing, query_grad)], 0
            )
            index = piece * blocks + block
            count = counts[index]
            listed = [lists[index * LIST + slot] for slot in range(LIST)]
            scores, weight_grads = [], []
            for slot in range(LIST):
                both = lax.dot_general(
                    window[listed[slot]],
                    operand,
                    (((1,), (1,)), ((), ())),
                    preferred_element_type=jnp.float32,
                )
                score = both[:, :BLK]
                if slot >= MIN_LIVE:
                    score = jnp.where(slot < count, score, -jnp.inf)
                scores.append(score)
                weight_grads.append(both[:, BLK:])
            top = jnp.max(functools.reduce(jnp.maximum, scores), axis=0, keepdims=True)
            raised = [jnp.exp2((score - top) * exponent_scale) for score in scores]
            row_sum = jnp.sum(functools.reduce(jnp.add, raised), axis=0, keepdims=True)
            products = [e * g for e, g in zip(raised, weight_grads)]
            row_dot = jnp.sum(functools.reduce(jnp.add, products), axis=0, keepdims=True)
            inverse = 1.0 / row_sum
            row_dot = row_dot * inverse
            for slot in range(LIST):
                span = slice(slot * BLK, (slot + 1) * BLK)
                pair[span, :BLK] = raised[slot].astype(jnp.bfloat16)
                pair[span, BLK:] = (raised[slot] * (weight_grads[slot] - row_dot)).astype(
                    jnp.bfloat16
                )
            listed_t = jnp.concatenate([window_t[listed[slot]] for slot in range(LIST)], axis=1)
            product = jnp.dot(listed_t, pair[...], preferred_element_type=jnp.float32)
            query_part = product[:HEAD_DIM, BLK:] * (inverse * score_scale)
            attended_part = product[HEAD_DIM:, :BLK] * inverse
            results[piece][0, rows, :] = (
                jnp.concatenate([query_part, attended_part], 0).T.astype(jnp.bfloat16)
            )
            scaled = query_grad.astype(jnp.float32) * jnp.broadcast_to(inverse, (BLK, BLK)).T
            blank = jnp.zeros_like(scaled)
            operand_back = jnp.concatenate(
                [jnp.where(left, blank, scaled), jnp.where(left, scaled * score_scale, blank)], 0
            ).astype(jnp.bfloat16)
            for slot in range(LIST):
                total[listed[slot]] += jnp.dot(
                    pair[slot * BLK : (slot + 1) * BLK, :],
                    operand_back,
                    preferred_element_type=jnp.float32,
                )
            return carry

        lax.fori_loop(0, blocks, query_block, 0)

    for piece in range(PIECES):
        for block in range(blocks):
            span = slice(block * BLK, (block + 1) * BLK)
            part = total[piece * blocks + block]
            if piece < QUAD:
                own[piece][0, span, :] = part
            elif piece < QUAD + 2:
                near[piece - QUAD, 0, span, :] = part.astype(jnp.bfloat16)
            else:
                far[piece - QUAD - 2, 0, span, :] = part.astype(jnp.bfloat16)


def attend(lists, counts, query_parts, key_parts):
    heads, rows, _ = query_parts[0].shape
    blocks = rows // BLK
    piece = pl.BlockSpec((1, rows, WIDE), lambda h, *_: (h, 0, 0))
    couple = pl.BlockSpec((2, 1, rows, WIDE), lambda h, *_: (0, h, 0, 0))
    shape = (heads, rows, WIDE)
    outs = pl.pallas_call(
        functools.partial(attend_body, blocks=blocks),
        grid_spec=pltpu.PrefetchScalarGridSpec(
            num_scalar_prefetch=2,
            grid=(heads,),
            in_specs=[piece] * (QUAD + PIECES),
            out_specs=[piece] * (2 * QUAD) + [couple] * 2,
            scratch_shapes=[
                pltpu.VMEM((PIECES * blocks, BLK, WIDE), jnp.bfloat16),
                pltpu.VMEM((PIECES * blocks, WIDE, BLK), jnp.bfloat16),
                pltpu.VMEM((PIECES * blocks, BLK, WIDE), jnp.float32),
                pltpu.VMEM((LIST * BLK, 2 * BLK), jnp.bfloat16),
            ],
        ),
        out_shape=[jax.ShapeDtypeStruct(shape, jnp.bfloat16)] * QUAD
        + [jax.ShapeDtypeStruct(shape, jnp.float32)] * QUAD
        + [jax.ShapeDtypeStruct((2,) + shape, jnp.bfloat16)] * 2,
        compiler_params=pltpu.CompilerParams(vmem_limit_bytes=VMEM_LIMIT),
        cost_estimate=pl.CostEstimate(
            flops=heads * QUAD * blocks * LIST * BLK * BLK * WIDE * 16,
            bytes_accessed=heads * rows * WIDE * 56,
            transcendentals=heads * QUAD * blocks * LIST * BLK * BLK,
        ),
        name="attend",
    )(lists, counts, *query_parts, *key_parts)
    return outs[:QUAD], outs[QUAD : 2 * QUAD], outs[2 * QUAD], outs[2 * QUAD + 1]


def combine_body(*refs):
    own, near, far, outs = refs[:QUAD], refs[QUAD], refs[QUAD + 1], refs[QUAD + 2 :]
    for piece in range(QUAD):
        other = near if piece < 2 else far
        outs[piece][0] = (own[piece][0] + other[piece % 2, 0].astype(jnp.float32)).astype(
            jnp.bfloat16
        )


def combine(own, near, far):
    heads, rows, _ = own[0].shape
    piece = pl.BlockSpec((1, rows, WIDE), lambda h: (h, 0, 0))
    couple = pl.BlockSpec((2, 1, rows, WIDE), lambda h: (0, h, 0, 0))
    return pl.pallas_call(
        combine_body,
        grid=(heads,),
        in_specs=[piece] * QUAD + [couple] * 2,
        out_specs=[piece] * QUAD,
        out_shape=[jax.ShapeDtypeStruct(own[0].shape, jnp.bfloat16)] * QUAD,
        compiler_params=pltpu.CompilerParams(vmem_limit_bytes=VMEM_LIMIT),
        cost_estimate=pl.CostEstimate(
            flops=0, bytes_accessed=heads * rows * WIDE * 32, transcendentals=0
        ),
        name="combine",
    )(*own, near, far)


def local(queries, key_rows, value_rows, out_grad, block_lists, list_counts):
    rows, width = queries.shape
    blocks = rows // BLK
    shards = lax.axis_size("tm")
    shard = lax.axis_index("tm")
    quad, place = shard // QUAD, shard % QUAD

    def across(x, flip):
        return lax.ppermute(x, "tm", [(i, i ^ flip) for i in range(shards)])

    def along(x, sign, flip=0):
        route = []
        for i in range(shards):
            j = i + (-QUAD if i % QUAD < 2 else QUAD) * sign
            if 0 <= j < shards:
                route.append((i, j ^ flip))
        return lax.ppermute(x, "tm", route)

    place_array = place.astype(jnp.int32).reshape(1)
    plan = jnp.concatenate([block_lists.reshape(-1), list_counts]).astype(jnp.int32)
    plans = jnp.stack([plan] + [across(plan, flip) for flip in range(1, QUAD)])
    listed = plans[:, : blocks * LIST].reshape(-1)
    counts = plans[:, blocks * LIST :].reshape(-1)
    owner = listed // blocks
    slots = ((owner % QUAD) ^ place) + jnp.where(owner // QUAD == quad, 0, QUAD)
    slots = slots * blocks + listed % blocks

    starts = [sum(CHUNKS[:n]) for n in range(len(CHUNKS))]
    packed = [
        pack(place_array, queries, out_grad, key_rows, value_rows, start, heads)
        for start, heads in zip(starts, CHUNKS)
    ]
    outs = None
    for start, (query_sent, key_sent) in zip(starts, packed):
        key_own = [key_sent[0]] + [across(key_sent[flip], flip) for flip in (1, 2, 3)]
        query_own = [query_sent[0]] + [across(query_sent[flip], flip) for flip in (1, 2, 3)]
        key_halo = [
            along(key_sent[0], 1),
            along(key_sent[1], 1, 1),
            along(key_own[2], -1),
            along(key_own[3], -1),
        ]
        results, own, near, far = attend(slots, counts, query_own, key_own + key_halo)
        near = along(near, -1)
        far = along(far, 1)
        sums = combine(own, near, far)
        query_back = [results[0]] + [across(results[flip], flip) for flip in (1, 2, 3)]
        key_back = [sums[0]] + [across(sums[flip], flip) for flip in (1, 2, 3)]
        outs = unpack(place_array, query_back, key_back, outs, start, width)
    query_grad, attended, key_grad, value_grad = outs
    return attended, query_grad, key_grad, value_grad


def solution(mesh):
    rows = P(("groups", "tm"), None)
    return jax.shard_map(
        local,
        mesh=mesh,
        in_specs=(rows, rows, rows, rows, rows, P(("groups", "tm"))),
        out_specs=(rows, rows, rows, rows),
        check_vma=False,
    )
```

```python
import functools
import math

import jax
import jax.numpy as jnp
from jax import lax
from jax.experimental import pallas as pl
from jax.experimental.pallas import tpu as pltpu
from jax.sharding import PartitionSpec as P

HEADS = 20
HEAD_DIM = 64
WIDE = 2 * HEAD_DIM
BLK = 128
LIST = 8
MIN_LIVE = 4
QUAD = 4
PIECES = 2 * QUAD
INS = (2, 2, 1)
OWNS = (2, 3)
OUTS = ((2, False), (2, False), (1, False))
COSTS = {"pack": 1.0, "gather": 0.5, "attend": 8.0, "combine": 0.3, "unpack": 0.8}
LOG2E = math.log2(math.e)
PACK_VMEM = 60 * 1024 * 1024
ATTEND_VMEM = 24 * 1024 * 1024
SMALL_VMEM = 12 * 1024 * 1024
PLAN_ROWS = 16
SPLIT = 128
ANYWHERE = pl.BlockSpec(memory_space=pl.ANY)


def cost(name, heads):
    return pl.CostEstimate(
        flops=int(COSTS[name] * heads * 1153e6), bytes_accessed=0, transcendentals=0
    )


def swapped(x):
    return jnp.concatenate([x[:, HEAD_DIM:], x[:, :HEAD_DIM]], axis=1)


def halves(first, second, core, left):
    low = jnp.where(left, first, swapped(second))
    high = jnp.where(left, swapped(first), second)
    return jnp.where(core == 0, low, high), jnp.where(core == 0, high, low)


def pair_columns(place, other):
    return pl.ds(pl.multiple_of((((place[0] // 2) % 2) ^ other) * WIDE, WIDE), WIDE)


def plan_rows(lists, counts):
    blocks = counts.shape[0]
    lane = lax.broadcasted_iota(jnp.int32, (PLAN_ROWS, WIDE), 1)
    row = lax.broadcasted_iota(jnp.int32, (PLAN_ROWS, WIDE), 0)
    values = jnp.zeros((PLAN_ROWS, WIDE), jnp.int32)
    for block in range(blocks):
        for slot in range(LIST):
            values = jnp.where(lane == block * LIST + slot, lists[block, slot], values)
        values = jnp.where(lane == blocks * LIST + block, counts[block], values)
    high = values // SPLIT
    return jnp.where(row == 0, values - high * SPLIT, jnp.where(row == 1, high, 0)).astype(jnp.float32)


def pack_body(place, lists, counts, *refs, heads, own, planned, after):
    sources, outs = refs[: 4 * heads], refs[4 * heads + after :]
    rows = sources[0].shape[0]
    left = lax.broadcasted_iota(jnp.int32, (rows, WIDE), 1) < HEAD_DIM
    plan = plan_rows(lists, counts).astype(jnp.bfloat16) if planned else None
    for h in range(heads):
        for kind in range(2):
            first, second = sources[4 * h + 2 * kind], sources[4 * h + 2 * kind + 1]
            pair = halves(first[...], second[...], place[0] % 2, left)
            if not own:
                outs[0][kind, h, :rows, :], outs[1][kind, h, :rows, :] = pair
            else:
                keys_ref, partner_ref, own_ref = outs
                partner_ref[kind, h, :rows, :] = pair[1]
                if kind == 0:
                    keys_ref[0, h], keys_ref[1, h] = pair
                else:
                    own_ref[0, h] = pair[0]
            if planned:
                for out in outs[1:2] if own else outs:
                    out[kind, h, rows:, :] = plan


def pack(scalars, arrays, start, heads, own, planned, after):
    rows = arrays[0].shape[0]

    def source(h):
        return pl.BlockSpec(
            (rows, WIDE),
            lambda _, place, *__: (0, 2 * (start + h) + (((place[0] // 2) % 2) ^ (0 if own else 1))),
        )

    shapes = [(2, heads, rows + PLAN_ROWS * planned, WIDE)] * 2
    if own:
        shapes = [(2, heads, rows, WIDE), shapes[0], (1, heads, rows, WIDE)]
    return pl.pallas_call(
        functools.partial(pack_body, heads=heads, own=own, planned=planned, after=len(after)),
        grid_spec=pltpu.PrefetchScalarGridSpec(
            num_scalar_prefetch=3,
            grid=(1,),
            in_specs=[source(h) for h in range(heads) for _ in range(4)] + [ANYWHERE] * len(after),
            out_specs=[pl.BlockSpec(shape, lambda *_: (0, 0, 0, 0)) for shape in shapes],
        ),
        out_shape=[jax.ShapeDtypeStruct(shape, jnp.bfloat16) for shape in shapes],
        compiler_params=pltpu.CompilerParams(vmem_limit_bytes=PACK_VMEM),
        cost_estimate=cost("pack", heads),
        name="pack",
    )(*scalars, *(arrays * heads), *after)


def follow_body(*refs):
    pass


def follow(x, after):
    return pl.pallas_call(
        follow_body,
        in_specs=[ANYWHERE] * 2,
        out_specs=ANYWHERE,
        out_shape=jax.ShapeDtypeStruct(x.shape, x.dtype),
        input_output_aliases={0: 0},
        compiler_params=pltpu.CompilerParams(vmem_limit_bytes=PACK_VMEM),
        name="follow",
    )(x, after)


def route_body(place, lists, counts, facing_ref, crossing_ref, partner_ref, out_ref):
    blocks = counts.shape[0]
    lane = lax.broadcasted_iota(jnp.int32, (1, WIDE), 1)
    own = plan_rows(lists, counts)
    for piece in range(QUAD):
        if piece == 0:
            rows = own
        else:
            source = (partner_ref, facing_ref, crossing_ref)[piece - 1]
            rows = source[0, 0].astype(jnp.float32)
        values = rows[0:1] + SPLIT * rows[1:2]
        owner = jnp.floor((values + 0.5) * (1.0 / blocks))
        quad = jnp.floor((owner + 0.5) * (1.0 / QUAD))
        inside = (owner - QUAD * quad).astype(jnp.int32) ^ (place[0] % QUAD)
        away = jnp.where(quad.astype(jnp.int32) == place[0] // QUAD, 0, QUAD)
        slots = (inside + away) * blocks + (values - blocks * owner).astype(jnp.int32)
        out_ref[piece : piece + 1, :] = jnp.where(
            lane < blocks * LIST, slots, values.astype(jnp.int32)
        )
    out_ref[QUAD:, :] = jnp.zeros((QUAD, WIDE), jnp.int32)


def route(scalars, facing, crossing, partner):
    rows = facing.shape[2] - PLAN_ROWS
    tail = pl.BlockSpec((1, 1, PLAN_ROWS, WIDE), lambda *_: (0, 0, rows // PLAN_ROWS, 0))
    return pl.pallas_call(
        route_body,
        grid_spec=pltpu.PrefetchScalarGridSpec(
            num_scalar_prefetch=3,
            grid=(1,),
            in_specs=[tail] * 3,
            out_specs=pl.BlockSpec((2 * QUAD, WIDE), lambda *_: (0, 0)),
        ),
        out_shape=jax.ShapeDtypeStruct((2 * QUAD, WIDE), jnp.int32),
        compiler_params=pltpu.CompilerParams(vmem_limit_bytes=SMALL_VMEM),
        cost_estimate=cost("gather", 1),
        name="route",
    )(*scalars, facing, crossing, partner)


def part(source, rows):
    _, index, first = source
    return pl.BlockSpec((1, 1, rows, WIDE), lambda h, *_: (index, first + h, 0, 0))


def unpack_body(place, *refs):
    parts, outs = refs[: 2 * QUAD], refs[-4:]
    core = place[0] % 2
    left = lax.broadcasted_iota(jnp.int32, (outs[0].shape[0], WIDE), 1) < HEAD_DIM
    for kind, (first_out, second_out) in enumerate((outs[:2], outs[2:])):
        for other in range(2):
            column = pair_columns(place, other)
            even = parts[kind * QUAD + 2 * other][0, 0]
            odd = parts[kind * QUAD + 2 * other + 1][0, 0]
            low = jnp.where(core == 0, even, odd)
            high = jnp.where(core == 0, odd, even)
            first_out[:, column] = jnp.where(left, low, swapped(high))
            second_out[:, column] = jnp.where(left, swapped(low), high)


def unpack(place, sources, so_far, start, heads, shape):
    rows, width = shape
    target = pl.BlockSpec((rows, 2 * WIDE), lambda h, _: (0, start + h))
    kept = [] if so_far is None else list(so_far)
    return pl.pallas_call(
        unpack_body,
        grid_spec=pltpu.PrefetchScalarGridSpec(
            num_scalar_prefetch=1,
            grid=(heads,),
            in_specs=[part(source, rows) for source in sources] + [ANYWHERE] * len(kept),
            out_specs=[target] * 4,
        ),
        out_shape=[jax.ShapeDtypeStruct(shape, jnp.bfloat16)] * 4,
        input_output_aliases={1 + 2 * QUAD + n: n for n in range(len(kept))},
        compiler_params=pltpu.CompilerParams(vmem_limit_bytes=SMALL_VMEM),
        cost_estimate=cost("unpack", heads),
        name="unpack",
    )(place, *[source[0] for source in sources], *kept)


def gather_body(facing_ref, crossing_ref, *refs):
    out_ref = refs[-1]
    out_ref[0, 0] = facing_ref[0, 0]
    out_ref[1, 0] = crossing_ref[0, 0]


def gather(facing, crossing, rows, after):
    heads = facing.shape[1]
    return pl.pallas_call(
        gather_body,
        grid=(heads,),
        in_specs=[part((facing, 0, 0), rows), part((crossing, 0, 0), rows)]
        + [ANYWHERE] * len(after),
        out_specs=pl.BlockSpec((2, 1, rows, WIDE), lambda h: (0, h, 0, 0)),
        out_shape=jax.ShapeDtypeStruct((2, heads, rows, WIDE), jnp.bfloat16),
        compiler_params=pltpu.CompilerParams(vmem_limit_bytes=SMALL_VMEM),
        cost_estimate=cost("gather", heads),
        name="gather",
    )(facing, crossing, *after)


def attend_body(plan, *refs, blocks, after):
    query_parts, key_parts = refs[:QUAD], refs[QUAD : QUAD + PIECES]
    refs = refs[QUAD + PIECES + after :]
    results, own, (near, far, window, window_t, total) = refs[:QUAD], refs[QUAD : 2 * QUAD], refs[2 * QUAD : 2 * QUAD + 5]
    products, pairs = refs[-4:-2], refs[-2:]
    score_scale = 1.0 / math.sqrt(HEAD_DIM)
    for piece in range(PIECES):
        for block in range(blocks):
            rows = key_parts[piece][0, 0, block * BLK : (block + 1) * BLK, :]
            window[piece * blocks + block] = rows
            window_t[piece * blocks + block] = rows.T
    total[...] = jnp.zeros_like(total)
    left = lax.broadcasted_iota(jnp.int32, (BLK, WIDE), 1) < HEAD_DIM
    upper = lax.broadcasted_iota(jnp.int32, (WIDE, BLK), 0) < HEAD_DIM
    spans = [slice(slot * BLK, (slot + 1) * BLK) for slot in range(LIST)]

    def listed(index):
        piece, block = divmod(index, blocks)
        return [plan[piece, block * LIST + slot] for slot in range(LIST)]

    def packed_rows(index):
        block = index % blocks
        return query_parts[index // blocks][0, 0, block * BLK : (block + 1) * BLK, :]

    def folded(combine_rows, x):
        return combine_rows(x.reshape(BLK // 8, 8, BLK), axis=0)

    tops, inverses = {}, {}

    def score(index):
        turned = packed_rows(index).T
        nothing = jnp.zeros_like(turned)
        operand = jnp.concatenate(
            [jnp.where(upper, turned, nothing), jnp.where(upper, nothing, turned)], axis=1
        )
        count = plan[index // blocks, blocks * LIST + index % blocks]
        product = products[index % 2]
        top = None
        for slot, block in enumerate(listed(index)):
            both = jnp.dot(window[block], operand, preferred_element_type=jnp.float32)
            scores = both[:, :BLK]
            if slot >= MIN_LIVE:
                scores = jnp.where(slot < count, scores, -jnp.inf)
            product[spans[slot], :BLK] = scores
            product[spans[slot], BLK:] = both[:, BLK:]
            here = folded(jnp.max, scores)
            top = here if top is None else jnp.maximum(top, here)
        tops[index] = top

    def soften(index):
        product, pair = products[index % 2], pairs[index % 2]
        top = jnp.max(tops.pop(index), axis=0, keepdims=True)
        row_sum = row_dot = jnp.zeros((8, BLK), jnp.float32)
        for span in spans:
            raised = jnp.exp2((product[span, :BLK] - top) * (LOG2E * score_scale))
            product[span, :BLK] = raised
            pair[span, :BLK] = raised.astype(jnp.bfloat16)
            row_sum += folded(jnp.sum, raised)
            row_dot += folded(jnp.sum, raised * product[span, BLK:])
        inverse = 1.0 / jnp.sum(row_sum, axis=0, keepdims=True)
        row_dot = jnp.sum(row_dot, axis=0, keepdims=True) * inverse
        for span in spans:
            pair[span, BLK:] = (product[span, :BLK] * (product[span, BLK:] - row_dot)).astype(
                jnp.bfloat16
            )
        inverses[index] = inverse

    def spread(index):
        pair, inverse = pairs[index % 2], inverses.pop(index)
        blocks_listed = listed(index)
        scaled = packed_rows(index).astype(jnp.float32) * jnp.broadcast_to(inverse, (BLK, BLK)).T
        blank = jnp.zeros_like(scaled)
        operand = jnp.concatenate(
            [jnp.where(left, blank, scaled), jnp.where(left, scaled * score_scale, blank)], 0
        ).astype(jnp.bfloat16)
        keys_t = jnp.concatenate([window_t[block] for block in blocks_listed], axis=1)
        product = jnp.dot(keys_t, pair[...], preferred_element_type=jnp.float32)
        query_part = product[:HEAD_DIM, BLK:] * (inverse * score_scale)
        attended_part = product[HEAD_DIM:, :BLK] * inverse
        block = index % blocks
        results[index // blocks][0, 0, block * BLK : (block + 1) * BLK, :] = (
            jnp.concatenate([query_part, attended_part], 0).astype(jnp.bfloat16).T
        )
        for span, block in zip(spans, blocks_listed):
            total[block] += jnp.dot(pair[span, :], operand, preferred_element_type=jnp.float32)

    count_all = QUAD * blocks
    for step in range(count_all + 2):
        if step >= 2:
            spread(step - 2)
        if 1 <= step <= count_all:
            soften(step - 1)
        if step < count_all:
            score(step)

    for piece in range(PIECES):
        for block in range(blocks):
            span = slice(block * BLK, (block + 1) * BLK)
            share = total[piece * blocks + block]
            if piece < QUAD:
                own[piece][0, span, :] = share
            elif piece < QUAD + 2:
                near[piece - QUAD, 0, span, :] = share.astype(jnp.bfloat16)
            else:
                far[piece - QUAD - 2, 0, span, :] = share.astype(jnp.bfloat16)


def attend(plan, sources, heads, split, after):
    rows = sources[0][0].shape[2]
    blocks = rows // BLK
    piece = pl.BlockSpec((1, rows, WIDE), lambda h, *_: (h, 0, 0))
    couple = pl.BlockSpec((2, 1, rows, WIDE), lambda h, *_: (0, h, 0, 0))
    shape = (heads, rows, WIDE)
    depth = 1 if split else 2
    result = part((None, depth - 1, 0), rows)
    outs = pl.pallas_call(
        functools.partial(attend_body, blocks=blocks, after=len(after)),
        grid_spec=pltpu.PrefetchScalarGridSpec(
            num_scalar_prefetch=1,
            grid=(heads,),
            in_specs=[part(source, rows) for source in sources] + [ANYWHERE] * len(after),
            out_specs=[result] * QUAD + [piece] * QUAD + [couple] * 2,
            scratch_shapes=[
                pltpu.VMEM((PIECES * blocks, BLK, WIDE), jnp.bfloat16),
                pltpu.VMEM((PIECES * blocks, WIDE, BLK), jnp.bfloat16),
                pltpu.VMEM((PIECES * blocks, BLK, WIDE), jnp.float32),
            ]
            + [pltpu.VMEM((LIST * BLK, 2 * BLK), jnp.float32)] * 2
            + [pltpu.VMEM((LIST * BLK, 2 * BLK), jnp.bfloat16)] * 2,
        ),
        out_shape=[jax.ShapeDtypeStruct((depth,) + shape, jnp.bfloat16)] * QUAD
        + [jax.ShapeDtypeStruct(shape, jnp.float32)] * QUAD
        + [jax.ShapeDtypeStruct((2,) + shape, jnp.bfloat16)] * 2,
        compiler_params=pltpu.CompilerParams(vmem_limit_bytes=ATTEND_VMEM),
        cost_estimate=cost("attend", heads),
        name="attend",
    )(plan, *[source[0] for source in sources], *after)
    return outs[:QUAD], outs[QUAD : 2 * QUAD], outs[2 * QUAD], outs[2 * QUAD + 1]


def combine_body(*refs):
    own, near, far, outs = refs[:QUAD], refs[QUAD], refs[QUAD + 1], refs[-QUAD:]
    for piece in range(QUAD):
        other = near if piece < 2 else far
        outs[piece][0, 0] = (own[piece][0] + other[piece % 2, 0].astype(jnp.float32)).astype(
            jnp.bfloat16
        )


def combine(own, near, far, results, after):
    heads, rows, _ = own[0].shape
    piece = pl.BlockSpec((1, rows, WIDE), lambda h: (h, 0, 0))
    couple = pl.BlockSpec((2, 1, rows, WIDE), lambda h: (0, h, 0, 0))
    shape = results[0].shape if results else (1, heads, rows, WIDE)
    return pl.pallas_call(
        combine_body,
        grid=(heads,),
        in_specs=[piece] * QUAD + [couple] * 2 + [ANYWHERE] * (len(results) + len(after)),
        out_specs=[part((None, 0, 0), rows)] * QUAD,
        out_shape=[jax.ShapeDtypeStruct(shape, jnp.bfloat16)] * QUAD,
        input_output_aliases={QUAD + 2 + n: n for n in range(len(results))},
        compiler_params=pltpu.CompilerParams(vmem_limit_bytes=SMALL_VMEM),
        cost_estimate=cost("combine", heads),
        name="combine",
    )(*own, near, far, *results, *after)


def started(sizes):
    return [sum(sizes[:n]) for n in range(len(sizes))]


def local(queries, key_rows, value_rows, out_grad, block_lists, list_counts):
    rows, width = queries.shape
    shards = lax.axis_size("tm")
    shard = lax.axis_index("tm")
    arrays = (key_rows, value_rows, queries, out_grad)

    def across(x, flip, name="lists"):
        with jax.named_scope(name):
            return lax.ppermute(x, "tm", [(i, i ^ flip) for i in range(shards)])

    def along(x, sign, name):
        route = []
        for i in range(shards):
            j = i + (-QUAD if i % QUAD < 2 else QUAD) * sign
            if 0 <= j < shards:
                route.append((i, j))
        with jax.named_scope(name):
            return lax.ppermute(x, "tm", route)

    def all_ways(parts, name):
        return [parts[0]] + [across(parts[flip], flip, name) for flip in (2, 3, 1)]

    scalars = (shard.astype(jnp.int32).reshape(1), block_lists, list_counts)
    ins, owns = [], []
    after = []
    for n, (start, heads) in enumerate(zip(started(INS), INS)):
        planned = n == 0
        facing, crossing = pack(scalars, arrays, start, heads, False, planned, after)
        after = [crossing]
        if n:
            facing, crossing = follow(facing, ins[-1][1]), follow(crossing, ins[-1][2])
        ins.append((start, across(facing, 2, f"facing{n}"), across(crossing, 3, f"crossing{n}")))
        if n < len(OWNS):
            start, heads = started(OWNS)[n], OWNS[n]
            keys, partner, query_own = pack(scalars, arrays, start, heads, True, planned, after)
            after = [partner]
            near = along(keys, 1, f"near{n}")
            partner = across(partner, 1, f"partner{n}")
            near_partner = across(near, 1, f"near_partner{n}")
            owns.append((start, keys, partner, query_own, near, near_partner))
    plan = route(scalars, ins[0][1], ins[0][2], owns[0][2])

    outs, fars, pending, previous, behind, ahead, earlier = None, {}, None, [], [], [], []
    calls = list(enumerate(zip(started([heads for heads, _ in OUTS]), OUTS)))
    for n, call in calls + [(len(calls), None)]:
        waiting, pending = pending, None
        if call is not None:
            start, (heads, split) = call
            first, keys, partner, query_own, near, near_partner = [
                o for o in owns if o[0] <= start
            ][-1]
            first = start - first
            later, facing, crossing = [i for i in ins if i[0] <= start][-1]
            if later not in fars:
                gathered = gather(facing, crossing, rows, earlier)
                fars[later] = along(gathered, -1, f"far{len(fars)}")
            far = fars[later]
            later = start - later
            sources = [
                (query_own, 0, first), (partner, 1, first), (facing, 1, later), (crossing, 1, later),
                (keys, 0, first), (partner, 0, first), (facing, 0, later), (crossing, 0, later),
                (near, 0, first), (near_partner, 1, first), (far, 0, later), (far, 1, later),
            ]
            results, own, near_back, far_back = attend(plan, sources, heads, split, previous + behind)
            earlier, previous = previous, [own[0]]
            if split:
                results = all_ways(results, f"results{n}")
            near_back = along(near_back, -1, f"near_back{n}")
            far_back = along(far_back, 1, f"far_back{n}")
            pending = (n, start, heads, split, results, own, near_back, far_back)
        if waiting is None:
            continue
        m, start, heads, split, results, own, near_back, far_back = waiting
        sums = combine(own, near_back, far_back, [] if split else results, (previous if call else []) + ahead)
        behind = [sums[0]]
        sums = all_ways(sums, f"sums{m}")
        ahead = sums[1:3] if m < len(OUTS) - 2 else []
        order = (0, 3, 1, 2)
        pieces = [(sums[k], 0, 0) for k in order]
        pieces += [(results[k], 0, 0) if split else (sums[k], 1, 0) for k in order]
        outs = unpack(scalars[0], pieces, outs, start, heads, (rows, width))
    key_grad, value_grad, query_grad, attended = outs
    return attended, query_grad, key_grad, value_grad


def solution(mesh):
    rows = P(("groups", "tm"), None)
    return jax.shard_map(
        local,
        mesh=mesh,
        in_specs=(rows, rows, rows, rows, rows, P(("groups", "tm"))),
        out_specs=(rows, rows, rows, rows),
        check_vma=False,
    )
```

```python
import functools
import math

import jax
import jax.numpy as jnp
from jax import lax
from jax.experimental import pallas as pl
from jax.experimental.pallas import tpu as pltpu
from jax.sharding import PartitionSpec as P

HEADS = 20
HEAD_DIM = 64
WIDE = 2 * HEAD_DIM
BLK = 128
LIST = 8
MIN_LIVE = 4
QUAD = 4
PIECES = 2 * QUAD
INS = (2, 1, 2)
OWNS = (2, 3)
OUTS = ((2, False), (1, False), (2, True))
COSTS = {"pack": 1.0, "gather": 0.5, "attend": 8.0, "combine": 0.3, "unpack": 0.8}
LOG2E = math.log2(math.e)
PACK_VMEM = 60 * 1024 * 1024
ATTEND_VMEM = 24 * 1024 * 1024
SMALL_VMEM = 12 * 1024 * 1024
PLAN_ROWS = 16
SPLIT = 128
ANYWHERE = pl.BlockSpec(memory_space=pl.ANY)


def cost(name, heads):
    return pl.CostEstimate(
        flops=int(COSTS[name] * heads * 1153e6), bytes_accessed=0, transcendentals=0
    )


def swapped(x):
    return jnp.concatenate([x[:, HEAD_DIM:], x[:, :HEAD_DIM]], axis=1)


def halves(first, second, core, left):
    low = jnp.where(left, first, swapped(second))
    high = jnp.where(left, swapped(first), second)
    return jnp.where(core == 0, low, high), jnp.where(core == 0, high, low)


def pair_columns(place, other):
    return pl.ds(pl.multiple_of((((place[0] // 2) % 2) ^ other) * WIDE, WIDE), WIDE)


def plan_rows(lists, counts):
    blocks = counts.shape[0]
    lane = lax.broadcasted_iota(jnp.int32, (PLAN_ROWS, WIDE), 1)
    row = lax.broadcasted_iota(jnp.int32, (PLAN_ROWS, WIDE), 0)
    values = jnp.zeros((PLAN_ROWS, WIDE), jnp.int32)
    for block in range(blocks):
        for slot in range(LIST):
            values = jnp.where(lane == block * LIST + slot, lists[block, slot], values)
        values = jnp.where(lane == blocks * LIST + block, counts[block], values)
    high = values // SPLIT
    return jnp.where(row == 0, values - high * SPLIT, jnp.where(row == 1, high, 0)).astype(jnp.float32)


def pack_body(place, lists, counts, *refs, heads, own, planned, after):
    sources, outs = refs[: 4 * heads], refs[4 * heads + after :]
    rows = sources[0].shape[0]
    left = lax.broadcasted_iota(jnp.int32, (rows, WIDE), 1) < HEAD_DIM
    plan = plan_rows(lists, counts).astype(jnp.bfloat16) if planned else None
    for h in range(heads):
        for kind in range(2):
            first, second = sources[4 * h + 2 * kind], sources[4 * h + 2 * kind + 1]
            pair = halves(first[...], second[...], place[0] % 2, left)
            if not own:
                outs[0][kind, h, :rows, :], outs[1][kind, h, :rows, :] = pair
            else:
                keys_ref, partner_ref, own_ref = outs
                partner_ref[kind, h, :rows, :] = pair[1]
                if kind == 0:
                    keys_ref[0, h], keys_ref[1, h] = pair
                else:
                    own_ref[0, h] = pair[0]
            if planned:
                for out in outs[1:2] if own else outs:
                    out[kind, h, rows:, :] = plan


def pack(scalars, arrays, start, heads, own, planned, after):
    rows = arrays[0].shape[0]

    def source(h):
        return pl.BlockSpec(
            (rows, WIDE),
            lambda _, place, *__: (0, 2 * (start + h) + (((place[0] // 2) % 2) ^ (0 if own else 1))),
        )

    shapes = [(2, heads, rows + PLAN_ROWS * planned, WIDE)] * 2
    if own:
        shapes = [(2, heads, rows, WIDE), shapes[0], (1, heads, rows, WIDE)]
    return pl.pallas_call(
        functools.partial(pack_body, heads=heads, own=own, planned=planned, after=len(after)),
        grid_spec=pltpu.PrefetchScalarGridSpec(
            num_scalar_prefetch=3,
            grid=(1,),
            in_specs=[source(h) for h in range(heads) for _ in range(4)] + [ANYWHERE] * len(after),
            out_specs=[pl.BlockSpec(shape, lambda *_: (0, 0, 0, 0)) for shape in shapes],
        ),
        out_shape=[jax.ShapeDtypeStruct(shape, jnp.bfloat16) for shape in shapes],
        compiler_params=pltpu.CompilerParams(vmem_limit_bytes=PACK_VMEM),
        cost_estimate=cost("pack", heads),
        name="pack",
    )(*scalars, *(arrays * heads), *after)


def follow_body(*refs):
    pass


def follow(x, after, vmem=PACK_VMEM):
    return pl.pallas_call(
        follow_body,
        in_specs=[ANYWHERE] * 2,
        out_specs=ANYWHERE,
        out_shape=jax.ShapeDtypeStruct(x.shape, x.dtype),
        input_output_aliases={0: 0},
        compiler_params=pltpu.CompilerParams(vmem_limit_bytes=vmem),
        name="follow",
    )(x, after)


def route_body(place, lists, counts, facing_ref, crossing_ref, partner_ref, out_ref):
    blocks = counts.shape[0]
    lane = lax.broadcasted_iota(jnp.int32, (1, WIDE), 1)
    own = plan_rows(lists, counts)
    for piece in range(QUAD):
        if piece == 0:
            rows = own
        else:
            source = (partner_ref, facing_ref, crossing_ref)[piece - 1]
            rows = source[0, 0].astype(jnp.float32)
        values = rows[0:1] + SPLIT * rows[1:2]
        owner = jnp.floor((values + 0.5) * (1.0 / blocks))
        quad = jnp.floor((owner + 0.5) * (1.0 / QUAD))
        inside = (owner - QUAD * quad).astype(jnp.int32) ^ (place[0] % QUAD)
        away = jnp.where(quad.astype(jnp.int32) == place[0] // QUAD, 0, QUAD)
        slots = (inside + away) * blocks + (values - blocks * owner).astype(jnp.int32)
        out_ref[piece : piece + 1, :] = jnp.where(
            lane < blocks * LIST, slots, values.astype(jnp.int32)
        )
    out_ref[QUAD:, :] = jnp.zeros((QUAD, WIDE), jnp.int32)


def route(scalars, facing, crossing, partner):
    rows = facing.shape[2] - PLAN_ROWS
    tail = pl.BlockSpec((1, 1, PLAN_ROWS, WIDE), lambda *_: (0, 0, rows // PLAN_ROWS, 0))
    return pl.pallas_call(
        route_body,
        grid_spec=pltpu.PrefetchScalarGridSpec(
            num_scalar_prefetch=3,
            grid=(1,),
            in_specs=[tail] * 3,
            out_specs=pl.BlockSpec((2 * QUAD, WIDE), lambda *_: (0, 0)),
        ),
        out_shape=jax.ShapeDtypeStruct((2 * QUAD, WIDE), jnp.int32),
        compiler_params=pltpu.CompilerParams(vmem_limit_bytes=SMALL_VMEM),
        cost_estimate=cost("gather", 1),
        name="route",
    )(*scalars, facing, crossing, partner)


def part(source, rows):
    _, index, first = source
    return pl.BlockSpec((1, 1, rows, WIDE), lambda h, *_: (index, first + h, 0, 0))


def unpack_body(place, *refs):
    parts, outs = refs[: 2 * QUAD], refs[-4:]
    core = place[0] % 2
    left = lax.broadcasted_iota(jnp.int32, (outs[0].shape[0], WIDE), 1) < HEAD_DIM
    for kind, (first_out, second_out) in enumerate((outs[:2], outs[2:])):
        for other in range(2):
            column = pair_columns(place, other)
            even = parts[kind * QUAD + 2 * other][0, 0]
            odd = parts[kind * QUAD + 2 * other + 1][0, 0]
            low = jnp.where(core == 0, even, odd)
            high = jnp.where(core == 0, odd, even)
            first_out[:, column] = jnp.where(left, low, swapped(high))
            second_out[:, column] = jnp.where(left, swapped(low), high)


def unpack(place, sources, so_far, start, heads, shape):
    rows, width = shape
    target = pl.BlockSpec((rows, 2 * WIDE), lambda h, _: (0, start + h))
    kept = [] if so_far is None else list(so_far)
    return pl.pallas_call(
        unpack_body,
        grid_spec=pltpu.PrefetchScalarGridSpec(
            num_scalar_prefetch=1,
            grid=(heads,),
            in_specs=[part(source, rows) for source in sources] + [ANYWHERE] * len(kept),
            out_specs=[target] * 4,
        ),
        out_shape=[jax.ShapeDtypeStruct(shape, jnp.bfloat16)] * 4,
        input_output_aliases={1 + 2 * QUAD + n: n for n in range(len(kept))},
        compiler_params=pltpu.CompilerParams(vmem_limit_bytes=SMALL_VMEM),
        cost_estimate=cost("unpack", heads),
        name="unpack",
    )(place, *[source[0] for source in sources], *kept)


def gather_body(facing_ref, crossing_ref, *refs):
    out_ref = refs[-1]
    out_ref[0, 0] = facing_ref[0, 0]
    out_ref[1, 0] = crossing_ref[0, 0]


def gather(facing, crossing, rows, after):
    heads = facing.shape[1]
    return pl.pallas_call(
        gather_body,
        grid=(heads,),
        in_specs=[part((facing, 0, 0), rows), part((crossing, 0, 0), rows)]
        + [ANYWHERE] * len(after),
        out_specs=pl.BlockSpec((2, 1, rows, WIDE), lambda h: (0, h, 0, 0)),
        out_shape=jax.ShapeDtypeStruct((2, heads, rows, WIDE), jnp.bfloat16),
        compiler_params=pltpu.CompilerParams(vmem_limit_bytes=SMALL_VMEM),
        cost_estimate=cost("gather", heads),
        name="gather",
    )(facing, crossing, *after)


def attend_body(plan, *refs, blocks, after):
    query_parts, key_parts = refs[:QUAD], refs[QUAD : QUAD + PIECES]
    refs = refs[QUAD + PIECES + after :]
    results, own, (near, far, window, window_t, total) = refs[:QUAD], refs[QUAD : 2 * QUAD], refs[2 * QUAD : 2 * QUAD + 5]
    products, pairs = refs[-4:-2], refs[-2:]
    score_scale = 1.0 / math.sqrt(HEAD_DIM)
    for piece in range(PIECES):
        for block in range(blocks):
            rows = key_parts[piece][0, 0, block * BLK : (block + 1) * BLK, :]
            window[piece * blocks + block] = rows
            window_t[piece * blocks + block] = rows.T
    total[...] = jnp.zeros_like(total)
    left = lax.broadcasted_iota(jnp.int32, (BLK, WIDE), 1) < HEAD_DIM
    upper = lax.broadcasted_iota(jnp.int32, (WIDE, BLK), 0) < HEAD_DIM
    spans = [slice(slot * BLK, (slot + 1) * BLK) for slot in range(LIST)]

    def listed(index):
        piece, block = divmod(index, blocks)
        return [plan[piece, block * LIST + slot] for slot in range(LIST)]

    def packed_rows(index):
        block = index % blocks
        return query_parts[index // blocks][0, 0, block * BLK : (block + 1) * BLK, :]

    def folded(combine_rows, x):
        return combine_rows(x.reshape(BLK // 8, 8, BLK), axis=0)

    tops, inverses = {}, {}

    def score(index):
        turned = packed_rows(index).T
        nothing = jnp.zeros_like(turned)
        operand = jnp.concatenate(
            [jnp.where(upper, turned, nothing), jnp.where(upper, nothing, turned)], axis=1
        )
        count = plan[index // blocks, blocks * LIST + index % blocks]
        product = products[index % 2]
        top = None
        for slot, block in enumerate(listed(index)):
            both = jnp.dot(window[block], operand, preferred_element_type=jnp.float32)
            scores = both[:, :BLK]
            if slot >= MIN_LIVE:
                scores = jnp.where(slot < count, scores, -jnp.inf)
            product[spans[slot], :BLK] = scores
            product[spans[slot], BLK:] = both[:, BLK:]
            here = folded(jnp.max, scores)
            top = here if top is None else jnp.maximum(top, here)
        tops[index] = top

    def soften(index):
        product, pair = products[index % 2], pairs[index % 2]
        top = jnp.max(tops.pop(index), axis=0, keepdims=True)
        row_sum = row_dot = jnp.zeros((8, BLK), jnp.float32)
        for span in spans:
            raised = jnp.exp2((product[span, :BLK] - top) * (LOG2E * score_scale))
            product[span, :BLK] = raised
            pair[span, :BLK] = raised.astype(jnp.bfloat16)
            row_sum += folded(jnp.sum, raised)
            row_dot += folded(jnp.sum, raised * product[span, BLK:])
        inverse = 1.0 / jnp.sum(row_sum, axis=0, keepdims=True)
        row_dot = jnp.sum(row_dot, axis=0, keepdims=True) * inverse
        for span in spans:
            pair[span, BLK:] = (product[span, :BLK] * (product[span, BLK:] - row_dot)).astype(
                jnp.bfloat16
            )
        inverses[index] = inverse

    def spread(index):
        pair, inverse = pairs[index % 2], inverses.pop(index)
        blocks_listed = listed(index)
        scaled = packed_rows(index).astype(jnp.float32) * jnp.broadcast_to(inverse, (BLK, BLK)).T
        blank = jnp.zeros_like(scaled)
        operand = jnp.concatenate(
            [jnp.where(left, blank, scaled), jnp.where(left, scaled * score_scale, blank)], 0
        ).astype(jnp.bfloat16)
        keys_t = jnp.concatenate([window_t[block] for block in blocks_listed], axis=1)
        product = jnp.dot(keys_t, pair[...], preferred_element_type=jnp.float32)
        query_part = product[:HEAD_DIM, BLK:] * (inverse * score_scale)
        attended_part = product[HEAD_DIM:, :BLK] * inverse
        block = index % blocks
        results[index // blocks][0, 0, block * BLK : (block + 1) * BLK, :] = (
            jnp.concatenate([query_part, attended_part], 0).astype(jnp.bfloat16).T
        )
        for span, block in zip(spans, blocks_listed):
            total[block] += jnp.dot(pair[span, :], operand, preferred_element_type=jnp.float32)

    count_all = QUAD * blocks
    for step in range(count_all + 2):
        if step >= 2:
            spread(step - 2)
        if 1 <= step <= count_all:
            soften(step - 1)
        if step < count_all:
            score(step)

    for piece in range(PIECES):
        for block in range(blocks):
            span = slice(block * BLK, (block + 1) * BLK)
            share = total[piece * blocks + block]
            if piece < QUAD:
                own[piece][0, span, :] = share
            elif piece < QUAD + 2:
                near[piece - QUAD, 0, span, :] = share.astype(jnp.bfloat16)
            else:
                far[piece - QUAD - 2, 0, span, :] = share.astype(jnp.bfloat16)


def attend(plan, sources, heads, split, after):
    rows = sources[0][0].shape[2]
    blocks = rows // BLK
    piece = pl.BlockSpec((1, rows, WIDE), lambda h, *_: (h, 0, 0))
    couple = pl.BlockSpec((2, 1, rows, WIDE), lambda h, *_: (0, h, 0, 0))
    shape = (heads, rows, WIDE)
    depth = 1 if split else 2
    result = part((None, depth - 1, 0), rows)
    outs = pl.pallas_call(
        functools.partial(attend_body, blocks=blocks, after=len(after)),
        grid_spec=pltpu.PrefetchScalarGridSpec(
            num_scalar_prefetch=1,
            grid=(heads,),
            in_specs=[part(source, rows) for source in sources] + [ANYWHERE] * len(after),
            out_specs=[result] * QUAD + [piece] * QUAD + [couple] * 2,
            scratch_shapes=[
                pltpu.VMEM((PIECES * blocks, BLK, WIDE), jnp.bfloat16),
                pltpu.VMEM((PIECES * blocks, WIDE, BLK), jnp.bfloat16),
                pltpu.VMEM((PIECES * blocks, BLK, WIDE), jnp.float32),
            ]
            + [pltpu.VMEM((LIST * BLK, 2 * BLK), jnp.float32)] * 2
            + [pltpu.VMEM((LIST * BLK, 2 * BLK), jnp.bfloat16)] * 2,
        ),
        out_shape=[jax.ShapeDtypeStruct((depth,) + shape, jnp.bfloat16)] * QUAD
        + [jax.ShapeDtypeStruct(shape, jnp.float32)] * QUAD
        + [jax.ShapeDtypeStruct((2,) + shape, jnp.bfloat16)] * 2,
        compiler_params=pltpu.CompilerParams(vmem_limit_bytes=ATTEND_VMEM),
        cost_estimate=cost("attend", heads),
        name="attend",
    )(plan, *[source[0] for source in sources], *after)
    return outs[:QUAD], outs[QUAD : 2 * QUAD], outs[2 * QUAD], outs[2 * QUAD + 1]


def combine_body(*refs):
    own, near, far, outs = refs[:QUAD], refs[QUAD], refs[QUAD + 1], refs[-QUAD:]
    for piece in range(QUAD):
        other = near if piece < 2 else far
        outs[piece][0, 0] = (own[piece][0] + other[piece % 2, 0].astype(jnp.float32)).astype(
            jnp.bfloat16
        )


def combine(own, near, far, results, after):
    heads, rows, _ = own[0].shape
    piece = pl.BlockSpec((1, rows, WIDE), lambda h: (h, 0, 0))
    couple = pl.BlockSpec((2, 1, rows, WIDE), lambda h: (0, h, 0, 0))
    shape = results[0].shape if results else (1, heads, rows, WIDE)
    return pl.pallas_call(
        combine_body,
        grid=(heads,),
        in_specs=[piece] * QUAD + [couple] * 2 + [ANYWHERE] * (len(results) + len(after)),
        out_specs=[part((None, 0, 0), rows)] * QUAD,
        out_shape=[jax.ShapeDtypeStruct(shape, jnp.bfloat16)] * QUAD,
        input_output_aliases={QUAD + 2 + n: n for n in range(len(results))},
        compiler_params=pltpu.CompilerParams(vmem_limit_bytes=SMALL_VMEM),
        cost_estimate=cost("combine", heads),
        name="combine",
    )(*own, near, far, *results, *after)


def started(sizes):
    return [sum(sizes[:n]) for n in range(len(sizes))]


def local(queries, key_rows, value_rows, out_grad, block_lists, list_counts):
    rows, width = queries.shape
    shards = lax.axis_size("tm")
    shard = lax.axis_index("tm")
    arrays = (key_rows, value_rows, queries, out_grad)

    def across(x, flip, name="lists"):
        with jax.named_scope(name):
            return lax.ppermute(x, "tm", [(i, i ^ flip) for i in range(shards)])

    def along(x, sign, name):
        route = []
        for i in range(shards):
            j = i + (-QUAD if i % QUAD < 2 else QUAD) * sign
            if 0 <= j < shards:
                route.append((i, j))
        with jax.named_scope(name):
            return lax.ppermute(x, "tm", route)

    def both_ways(parts, name):
        return [across(parts[flip], flip, name) for flip in (2, 3)]

    def all_ways(parts, after, name):
        far_parts = both_ways(parts, name)
        return [parts[0]] + far_parts + [across(follow(parts[1], after, SMALL_VMEM), 1, name)]

    scalars = (shard.astype(jnp.int32).reshape(1), block_lists, list_counts)
    ins, owns = [], []
    after = []
    for n, (start, heads) in enumerate(zip(started(INS), INS)):
        planned = n == 0
        facing, crossing = pack(scalars, arrays, start, heads, False, planned, after)
        after = [crossing]
        if n:
            facing, crossing = follow(facing, ins[-1][1]), follow(crossing, ins[-1][2])
        ins.append((start, across(facing, 2, f"facing{n}"), across(crossing, 3, f"crossing{n}")))
        if n < len(OWNS):
            start, heads = started(OWNS)[n], OWNS[n]
            keys, partner, query_own = pack(scalars, arrays, start, heads, True, planned, after)
            after = [partner]
            near = along(keys, 1, f"near{n}")
            partner = across(partner, 1, f"partner{n}")
            near_partner = across(near, 1, f"near_partner{n}")
            owns.append((start, keys, partner, query_own, near, near_partner))
    plan = route(scalars, ins[0][1], ins[0][2], owns[0][2])

    outs, fars, pending, previous, behind, ahead, earlier = None, {}, None, [], [], [], []
    arrived = []
    calls = list(enumerate(zip(started([heads for heads, _ in OUTS]), OUTS)))
    for n, call in calls + [(len(calls), None)]:
        waiting, pending = pending, None
        if call is not None:
            start, (heads, split) = call
            first, keys, partner, query_own, near, near_partner = [
                o for o in owns if o[0] <= start
            ][-1]
            first = start - first
            later, facing, crossing = [i for i in ins if i[0] <= start][-1]
            if later not in fars:
                gathered = gather(facing, crossing, rows, previous if n == 1 else earlier)
                fars[later] = along(gathered, -1, f"far{len(fars)}")
            far = fars[later]
            later = start - later
            sources = [
                (query_own, 0, first), (partner, 1, first), (facing, 1, later), (crossing, 1, later),
                (keys, 0, first), (partner, 0, first), (facing, 0, later), (crossing, 0, later),
                (near, 0, first), (near_partner, 1, first), (far, 0, later), (far, 1, later),
            ]
            results, own, near_back, far_back = attend(plan, sources, heads, split, previous + behind)
            earlier, previous = previous, [own[0]]
            near_back = along(near_back, -1, f"near_back{n}")
            if split:
                results = all_ways(results, near_back, f"results{n}")
            far_back = along(far_back, 1, f"far_back{n}")
            pending = (n, start, heads, split, results, own, near_back, far_back)
        if waiting is None:
            continue
        m, start, heads, split, results, own, near_back, far_back = waiting
        sums = combine(own, near_back, far_back, [] if split else results, (previous if call else []) + ahead)
        behind = [sums[0]]
        sent = both_ways(sums, f"sums{m}")
        ahead = sent if m < len(OUTS) - 2 else []
        arrived.append((start, heads, split, results, [sums[0]] + sent, sums[1]))
    for m, (start, heads, split, results, sums, partner) in enumerate(arrived):
        if m < len(arrived) - 1:
            partner = follow(partner, previous[0], SMALL_VMEM)
        sums = sums + [across(partner, 1, f"sums_partner{m}")]
        order = (0, 3, 1, 2)
        pieces = [(sums[k], 0, 0) for k in order]
        pieces += [(results[k], 0, 0) if split else (sums[k], 1, 0) for k in order]
        outs = unpack(scalars[0], pieces, outs, start, heads, (rows, width))
    key_grad, value_grad, query_grad, attended = outs
    return attended, query_grad, key_grad, value_grad


def solution(mesh):
    rows = P(("groups", "tm"), None)
    return jax.shard_map(
        local,
        mesh=mesh,
        in_specs=(rows, rows, rows, rows, rows, P(("groups", "tm"))),
        out_specs=(rows, rows, rows, rows),
        check_vma=False,
    )
```

```python
import functools
import math

import jax
import jax.numpy as jnp
from jax import lax
from jax.experimental import pallas as pl
from jax.experimental.pallas import tpu as pltpu
from jax.sharding import PartitionSpec as P

HEADS = 20
HEAD_DIM = 64
WIDE = 2 * HEAD_DIM
BLK = 128
LIST = 8
MIN_LIVE = 4
QUAD = 4
PIECES = 2 * QUAD
INS = (2, 2, 1)
OWNS = (2, 3)
OUTS = ((2, False), (2, False), (1, False))
COSTS = {"pack": 1.0, "gather": 0.5, "attend": 8.0, "combine": 0.3, "unpack": 0.8}
LOG2E = math.log2(math.e)
PACK_VMEM = 60 * 1024 * 1024
ATTEND_VMEM = 24 * 1024 * 1024
SMALL_VMEM = 12 * 1024 * 1024
PLAN_ROWS = 16
SPLIT = 128
ANYWHERE = pl.BlockSpec(memory_space=pl.ANY)


def cost(name, heads):
    return pl.CostEstimate(
        flops=int(COSTS[name] * heads * 1153e6), bytes_accessed=0, transcendentals=0
    )


def swapped(x):
    return jnp.concatenate([x[:, HEAD_DIM:], x[:, :HEAD_DIM]], axis=1)


def halves(first, second, core, left):
    low = jnp.where(left, first, swapped(second))
    high = jnp.where(left, swapped(first), second)
    return jnp.where(core == 0, low, high), jnp.where(core == 0, high, low)


def pair_columns(place, other):
    return pl.ds(pl.multiple_of((((place[0] // 2) % 2) ^ other) * WIDE, WIDE), WIDE)


def plan_rows(lists, counts):
    blocks = counts.shape[0]
    lane = lax.broadcasted_iota(jnp.int32, (PLAN_ROWS, WIDE), 1)
    row = lax.broadcasted_iota(jnp.int32, (PLAN_ROWS, WIDE), 0)
    values = jnp.zeros((PLAN_ROWS, WIDE), jnp.int32)
    for block in range(blocks):
        for slot in range(LIST):
            values = jnp.where(lane == block * LIST + slot, lists[block, slot], values)
        values = jnp.where(lane == blocks * LIST + block, counts[block], values)
    high = values // SPLIT
    return jnp.where(row == 0, values - high * SPLIT, jnp.where(row == 1, high, 0)).astype(jnp.float32)


def pack_body(place, lists, counts, *refs, heads, own, planned, after):
    sources, outs = refs[: 4 * heads], refs[4 * heads + after :]
    rows = sources[0].shape[0]
    left = lax.broadcasted_iota(jnp.int32, (rows, WIDE), 1) < HEAD_DIM
    plan = plan_rows(lists, counts).astype(jnp.bfloat16) if planned else None
    for h in range(heads):
        for kind in range(2):
            first, second = sources[4 * h + 2 * kind], sources[4 * h + 2 * kind + 1]
            pair = halves(first[...], second[...], place[0] % 2, left)
            if not own:
                outs[0][kind, h, :rows, :], outs[1][kind, h, :rows, :] = pair
            else:
                keys_ref, partner_ref, own_ref = outs
                partner_ref[kind, h, :rows, :] = pair[1]
                if kind == 0:
                    keys_ref[0, h], keys_ref[1, h] = pair
                else:
                    own_ref[0, h] = pair[0]
            if planned:
                for out in outs[1:2] if own else outs:
                    out[kind, h, rows:, :] = plan


def pack(scalars, arrays, start, heads, own, planned, after):
    rows = arrays[0].shape[0]

    def source(h):
        return pl.BlockSpec(
            (rows, WIDE),
            lambda _, place, *__: (0, 2 * (start + h) + (((place[0] // 2) % 2) ^ (0 if own else 1))),
        )

    shapes = [(2, heads, rows + PLAN_ROWS * planned, WIDE)] * 2
    if own:
        shapes = [(2, heads, rows, WIDE), shapes[0], (1, heads, rows, WIDE)]
    return pl.pallas_call(
        functools.partial(pack_body, heads=heads, own=own, planned=planned, after=len(after)),
        grid_spec=pltpu.PrefetchScalarGridSpec(
            num_scalar_prefetch=3,
            grid=(1,),
            in_specs=[source(h) for h in range(heads) for _ in range(4)] + [ANYWHERE] * len(after),
            out_specs=[pl.BlockSpec(shape, lambda *_: (0, 0, 0, 0)) for shape in shapes],
        ),
        out_shape=[jax.ShapeDtypeStruct(shape, jnp.bfloat16) for shape in shapes],
        compiler_params=pltpu.CompilerParams(vmem_limit_bytes=PACK_VMEM),
        cost_estimate=cost("pack", heads),
        name="pack",
    )(*scalars, *(arrays * heads), *after)


def follow_body(*refs):
    pass


def follow(x, after, vmem=PACK_VMEM):
    return pl.pallas_call(
        follow_body,
        in_specs=[ANYWHERE] * 2,
        out_specs=ANYWHERE,
        out_shape=jax.ShapeDtypeStruct(x.shape, x.dtype),
        input_output_aliases={0: 0},
        compiler_params=pltpu.CompilerParams(vmem_limit_bytes=vmem),
        name="follow",
    )(x, after)


def route_body(place, lists, counts, facing_ref, crossing_ref, partner_ref, out_ref):
    blocks = counts.shape[0]
    lane = lax.broadcasted_iota(jnp.int32, (1, WIDE), 1)
    own = plan_rows(lists, counts)
    for piece in range(QUAD):
        if piece == 0:
            rows = own
        else:
            source = (partner_ref, facing_ref, crossing_ref)[piece - 1]
            rows = source[0, 0].astype(jnp.float32)
        values = rows[0:1] + SPLIT * rows[1:2]
        owner = jnp.floor((values + 0.5) * (1.0 / blocks))
        quad = jnp.floor((owner + 0.5) * (1.0 / QUAD))
        inside = (owner - QUAD * quad).astype(jnp.int32) ^ (place[0] % QUAD)
        away = jnp.where(quad.astype(jnp.int32) == place[0] // QUAD, 0, QUAD)
        slots = (inside + away) * blocks + (values - blocks * owner).astype(jnp.int32)
        out_ref[piece : piece + 1, :] = jnp.where(
            lane < blocks * LIST, slots, values.astype(jnp.int32)
        )
    out_ref[QUAD:, :] = jnp.zeros((QUAD, WIDE), jnp.int32)


def route(scalars, facing, crossing, partner):
    rows = facing.shape[2] - PLAN_ROWS
    tail = pl.BlockSpec((1, 1, PLAN_ROWS, WIDE), lambda *_: (0, 0, rows // PLAN_ROWS, 0))
    return pl.pallas_call(
        route_body,
        grid_spec=pltpu.PrefetchScalarGridSpec(
            num_scalar_prefetch=3,
            grid=(1,),
            in_specs=[tail] * 3,
            out_specs=pl.BlockSpec((2 * QUAD, WIDE), lambda *_: (0, 0)),
        ),
        out_shape=jax.ShapeDtypeStruct((2 * QUAD, WIDE), jnp.int32),
        compiler_params=pltpu.CompilerParams(vmem_limit_bytes=SMALL_VMEM),
        cost_estimate=cost("gather", 1),
        name="route",
    )(*scalars, facing, crossing, partner)


def part(source, rows):
    _, index, first = source
    return pl.BlockSpec((1, 1, rows, WIDE), lambda h, *_: (index, first + h, 0, 0))


def unpack_body(place, *refs):
    parts, outs = refs[: 2 * QUAD], refs[-4:]
    core = place[0] % 2
    left = lax.broadcasted_iota(jnp.int32, (outs[0].shape[0], WIDE), 1) < HEAD_DIM
    for kind, (first_out, second_out) in enumerate((outs[:2], outs[2:])):
        for other in range(2):
            column = pair_columns(place, other)
            even = parts[kind * QUAD + 2 * other][0, 0]
            odd = parts[kind * QUAD + 2 * other + 1][0, 0]
            low = jnp.where(core == 0, even, odd)
            high = jnp.where(core == 0, odd, even)
            first_out[:, column] = jnp.where(left, low, swapped(high))
            second_out[:, column] = jnp.where(left, swapped(low), high)


def unpack(place, sources, so_far, start, heads, shape):
    rows, width = shape
    target = pl.BlockSpec((rows, 2 * WIDE), lambda h, _: (0, start + h))
    kept = [] if so_far is None else list(so_far)
    return pl.pallas_call(
        unpack_body,
        grid_spec=pltpu.PrefetchScalarGridSpec(
            num_scalar_prefetch=1,
            grid=(heads,),
            in_specs=[part(source, rows) for source in sources] + [ANYWHERE] * len(kept),
            out_specs=[target] * 4,
        ),
        out_shape=[jax.ShapeDtypeStruct(shape, jnp.bfloat16)] * 4,
        input_output_aliases={1 + 2 * QUAD + n: n for n in range(len(kept))},
        compiler_params=pltpu.CompilerParams(vmem_limit_bytes=SMALL_VMEM),
        cost_estimate=cost("unpack", heads),
        name="unpack",
    )(place, *[source[0] for source in sources], *kept)


def gather_body(facing_ref, crossing_ref, *refs):
    out_ref = refs[-1]
    out_ref[0, 0] = facing_ref[0, 0]
    out_ref[1, 0] = crossing_ref[0, 0]


def gather(facing, crossing, rows, after):
    heads = facing.shape[1]
    return pl.pallas_call(
        gather_body,
        grid=(heads,),
        in_specs=[part((facing, 0, 0), rows), part((crossing, 0, 0), rows)]
        + [ANYWHERE] * len(after),
        out_specs=pl.BlockSpec((2, 1, rows, WIDE), lambda h: (0, h, 0, 0)),
        out_shape=jax.ShapeDtypeStruct((2, heads, rows, WIDE), jnp.bfloat16),
        compiler_params=pltpu.CompilerParams(vmem_limit_bytes=SMALL_VMEM),
        cost_estimate=cost("gather", heads),
        name="gather",
    )(facing, crossing, *after)


def attend_body(plan, *refs, blocks, after):
    query_parts, key_parts = refs[:QUAD], refs[QUAD : QUAD + PIECES]
    refs = refs[QUAD + PIECES + after :]
    results, own, (near, far, window, window_t, total) = refs[:QUAD], refs[QUAD : 2 * QUAD], refs[2 * QUAD : 2 * QUAD + 5]
    products, pairs = refs[-4:-2], refs[-2:]
    score_scale = 1.0 / math.sqrt(HEAD_DIM)
    for piece in range(PIECES):
        for block in range(blocks):
            rows = key_parts[piece][0, 0, block * BLK : (block + 1) * BLK, :]
            window[piece * blocks + block] = rows
            window_t[piece * blocks + block] = rows.T
    total[...] = jnp.zeros_like(total)
    left = lax.broadcasted_iota(jnp.int32, (BLK, WIDE), 1) < HEAD_DIM
    upper = lax.broadcasted_iota(jnp.int32, (WIDE, BLK), 0) < HEAD_DIM
    spans = [slice(slot * BLK, (slot + 1) * BLK) for slot in range(LIST)]

    def listed(index):
        piece, block = divmod(index, blocks)
        return [plan[piece, block * LIST + slot] for slot in range(LIST)]

    def packed_rows(index):
        block = index % blocks
        return query_parts[index // blocks][0, 0, block * BLK : (block + 1) * BLK, :]

    def folded(combine_rows, x):
        return combine_rows(x.reshape(BLK // 8, 8, BLK), axis=0)

    tops, inverses = {}, {}

    def score(index):
        turned = packed_rows(index).T
        nothing = jnp.zeros_like(turned)
        operand = jnp.concatenate(
            [jnp.where(upper, turned, nothing), jnp.where(upper, nothing, turned)], axis=1
        )
        count = plan[index // blocks, blocks * LIST + index % blocks]
        product = products[index % 2]
        top = None
        for slot, block in enumerate(listed(index)):
            both = jnp.dot(window[block], operand, preferred_element_type=jnp.float32)
            scores = both[:, :BLK]
            if slot >= MIN_LIVE:
                scores = jnp.where(slot < count, scores, -jnp.inf)
            product[spans[slot], :BLK] = scores
            product[spans[slot], BLK:] = both[:, BLK:]
            here = folded(jnp.max, scores)
            top = here if top is None else jnp.maximum(top, here)
        tops[index] = top

    def soften(index):
        product, pair = products[index % 2], pairs[index % 2]
        top = jnp.max(tops.pop(index), axis=0, keepdims=True)
        row_sum = row_dot = jnp.zeros((8, BLK), jnp.float32)
        for span in spans:
            raised = jnp.exp2((product[span, :BLK] - top) * (LOG2E * score_scale))
            product[span, :BLK] = raised
            pair[span, :BLK] = raised.astype(jnp.bfloat16)
            row_sum += folded(jnp.sum, raised)
            row_dot += folded(jnp.sum, raised * product[span, BLK:])
        inverse = 1.0 / jnp.sum(row_sum, axis=0, keepdims=True)
        row_dot = jnp.sum(row_dot, axis=0, keepdims=True) * inverse
        for span in spans:
            pair[span, BLK:] = (product[span, :BLK] * (product[span, BLK:] - row_dot)).astype(
                jnp.bfloat16
            )
        inverses[index] = inverse

    def spread(index):
        pair, inverse = pairs[index % 2], inverses.pop(index)
        blocks_listed = listed(index)
        scaled = packed_rows(index).astype(jnp.float32) * jnp.broadcast_to(inverse, (BLK, BLK)).T
        blank = jnp.zeros_like(scaled)
        operand = jnp.concatenate(
            [jnp.where(left, blank, scaled), jnp.where(left, scaled * score_scale, blank)], 0
        ).astype(jnp.bfloat16)
        keys_t = jnp.concatenate([window_t[block] for block in blocks_listed], axis=1)
        product = jnp.dot(keys_t, pair[...], preferred_element_type=jnp.float32)
        query_part = product[:HEAD_DIM, BLK:] * (inverse * score_scale)
        attended_part = product[HEAD_DIM:, :BLK] * inverse
        block = index % blocks
        results[index // blocks][0, 0, block * BLK : (block + 1) * BLK, :] = (
            jnp.concatenate([query_part, attended_part], 0).astype(jnp.bfloat16).T
        )
        for span, block in zip(spans, blocks_listed):
            total[block] += jnp.dot(pair[span, :], operand, preferred_element_type=jnp.float32)

    count_all = QUAD * blocks
    for step in range(count_all + 2):
        if step >= 2:
            spread(step - 2)
        if 1 <= step <= count_all:
            soften(step - 1)
        if step < count_all:
            score(step)

    for piece in range(PIECES):
        for block in range(blocks):
            span = slice(block * BLK, (block + 1) * BLK)
            share = total[piece * blocks + block]
            if piece < QUAD:
                own[piece][0, span, :] = share
            elif piece < QUAD + 2:
                near[piece - QUAD, 0, span, :] = share.astype(jnp.bfloat16)
            else:
                far[piece - QUAD - 2, 0, span, :] = share.astype(jnp.bfloat16)


def attend(plan, sources, heads, split, after):
    rows = sources[0][0].shape[2]
    blocks = rows // BLK
    piece = pl.BlockSpec((1, rows, WIDE), lambda h, *_: (h, 0, 0))
    couple = pl.BlockSpec((2, 1, rows, WIDE), lambda h, *_: (0, h, 0, 0))
    shape = (heads, rows, WIDE)
    depth = 1 if split else 2
    result = part((None, depth - 1, 0), rows)
    outs = pl.pallas_call(
        functools.partial(attend_body, blocks=blocks, after=len(after)),
        grid_spec=pltpu.PrefetchScalarGridSpec(
            num_scalar_prefetch=1,
            grid=(heads,),
            in_specs=[part(source, rows) for source in sources] + [ANYWHERE] * len(after),
            out_specs=[result] * QUAD + [piece] * QUAD + [couple] * 2,
            scratch_shapes=[
                pltpu.VMEM((PIECES * blocks, BLK, WIDE), jnp.bfloat16),
                pltpu.VMEM((PIECES * blocks, WIDE, BLK), jnp.bfloat16),
                pltpu.VMEM((PIECES * blocks, BLK, WIDE), jnp.float32),
            ]
            + [pltpu.VMEM((LIST * BLK, 2 * BLK), jnp.float32)] * 2
            + [pltpu.VMEM((LIST * BLK, 2 * BLK), jnp.bfloat16)] * 2,
        ),
        out_shape=[jax.ShapeDtypeStruct((depth,) + shape, jnp.bfloat16)] * QUAD
        + [jax.ShapeDtypeStruct(shape, jnp.float32)] * QUAD
        + [jax.ShapeDtypeStruct((2,) + shape, jnp.bfloat16)] * 2,
        compiler_params=pltpu.CompilerParams(vmem_limit_bytes=ATTEND_VMEM),
        cost_estimate=cost("attend", heads),
        name="attend",
    )(plan, *[source[0] for source in sources], *after)
    return outs[:QUAD], outs[QUAD : 2 * QUAD], outs[2 * QUAD], outs[2 * QUAD + 1]


def combine_body(*refs):
    own, near, far, outs = refs[:QUAD], refs[QUAD], refs[QUAD + 1], refs[-QUAD:]
    for piece in range(QUAD):
        other = near if piece < 2 else far
        outs[piece][0, 0] = (own[piece][0] + other[piece % 2, 0].astype(jnp.float32)).astype(
            jnp.bfloat16
        )


def combine(own, near, far, results, after):
    heads, rows, _ = own[0].shape
    piece = pl.BlockSpec((1, rows, WIDE), lambda h: (h, 0, 0))
    couple = pl.BlockSpec((2, 1, rows, WIDE), lambda h: (0, h, 0, 0))
    shape = results[0].shape if results else (1, heads, rows, WIDE)
    return pl.pallas_call(
        combine_body,
        grid=(heads,),
        in_specs=[piece] * QUAD + [couple] * 2 + [ANYWHERE] * (len(results) + len(after)),
        out_specs=[part((None, 0, 0), rows)] * QUAD,
        out_shape=[jax.ShapeDtypeStruct(shape, jnp.bfloat16)] * QUAD,
        input_output_aliases={QUAD + 2 + n: n for n in range(len(results))},
        compiler_params=pltpu.CompilerParams(vmem_limit_bytes=SMALL_VMEM),
        cost_estimate=cost("combine", heads),
        name="combine",
    )(*own, near, far, *results, *after)


def started(sizes):
    return [sum(sizes[:n]) for n in range(len(sizes))]


def local(queries, key_rows, value_rows, out_grad, block_lists, list_counts):
    rows, width = queries.shape
    shards = lax.axis_size("tm")
    shard = lax.axis_index("tm")
    arrays = (key_rows, value_rows, queries, out_grad)

    def across(x, flip, name="lists"):
        with jax.named_scope(name):
            return lax.ppermute(x, "tm", [(i, i ^ flip) for i in range(shards)])

    def along(x, sign, name):
        route = []
        for i in range(shards):
            j = i + (-QUAD if i % QUAD < 2 else QUAD) * sign
            if 0 <= j < shards:
                route.append((i, j))
        with jax.named_scope(name):
            return lax.ppermute(x, "tm", route)

    def both_ways(parts, name):
        return [across(parts[flip], flip, name) for flip in (2, 3)]

    def all_ways(parts, after, name):
        far_parts = both_ways(parts, name)
        return [parts[0]] + far_parts + [across(follow(parts[1], after, SMALL_VMEM), 1, name)]

    scalars = (shard.astype(jnp.int32).reshape(1), block_lists, list_counts)
    ins, owns = [], []
    after = []
    for n, (start, heads) in enumerate(zip(started(INS), INS)):
        planned = n == 0
        facing, crossing = pack(scalars, arrays, start, heads, False, planned, after)
        after = [crossing]
        if n:
            facing, crossing = follow(facing, ins[-1][1]), follow(crossing, ins[-1][2])
        ins.append((start, across(facing, 2, f"facing{n}"), across(crossing, 3, f"crossing{n}")))
        if n < len(OWNS):
            start, heads = started(OWNS)[n], OWNS[n]
            keys, partner, query_own = pack(scalars, arrays, start, heads, True, planned, after)
            after = [partner]
            near = along(keys, 1, f"near{n}")
            partner = across(partner, 1, f"partner{n}")
            near_partner = across(near, 1, f"near_partner{n}")
            owns.append((start, keys, partner, query_own, near, near_partner))
    plan = route(scalars, ins[0][1], ins[0][2], owns[0][2])

    outs, fars, pending, previous, behind, ahead, earlier = None, {}, None, [], [], [], []
    arrived = []
    calls = list(enumerate(zip(started([heads for heads, _ in OUTS]), OUTS)))
    for n, call in calls + [(len(calls), None)]:
        waiting, pending = pending, None
        if call is not None:
            start, (heads, split) = call
            first, keys, partner, query_own, near, near_partner = [
                o for o in owns if o[0] <= start
            ][-1]
            first = start - first
            later, facing, crossing = [i for i in ins if i[0] <= start][-1]
            if later not in fars:
                gathered = gather(facing, crossing, rows, previous if n == 1 else earlier)
                fars[later] = along(gathered, -1, f"far{len(fars)}")
            far = fars[later]
            later = start - later
            sources = [
                (query_own, 0, first), (partner, 1, first), (facing, 1, later), (crossing, 1, later),
                (keys, 0, first), (partner, 0, first), (facing, 0, later), (crossing, 0, later),
                (near, 0, first), (near_partner, 1, first), (far, 0, later), (far, 1, later),
            ]
            results, own, near_back, far_back = attend(plan, sources, heads, split, previous + behind)
            earlier, previous = previous, [own[0]]
            near_back = along(near_back, -1, f"near_back{n}")
            if split:
                results = all_ways(results, near_back, f"results{n}")
            far_back = along(far_back, 1, f"far_back{n}")
            pending = (n, start, heads, split, results, own, near_back, far_back)
        if waiting is None:
            continue
        m, start, heads, split, results, own, near_back, far_back = waiting
        sums = combine(own, near_back, far_back, [] if split else results, (previous if call else []) + ahead)
        behind = [sums[0]]
        sent = both_ways(sums, f"sums{m}")
        ahead = sent if m < len(OUTS) - 2 else []
        arrived.append((start, heads, split, results, [sums[0]] + sent, sums[1]))
    for m, (start, heads, split, results, sums, partner) in enumerate(arrived):
        if m < len(arrived) - 1:
            partner = follow(partner, previous[0], SMALL_VMEM)
        sums = sums + [across(partner, 1, f"sums_partner{m}")]
        order = (0, 3, 1, 2)
        pieces = [(sums[k], 0, 0) for k in order]
        pieces += [(results[k], 0, 0) if split else (sums[k], 1, 0) for k in order]
        outs = unpack(scalars[0], pieces, outs, start, heads, (rows, width))
    key_grad, value_grad, query_grad, attended = outs
    return attended, query_grad, key_grad, value_grad


def solution(mesh):
    rows = P(("groups", "tm"), None)
    return jax.shard_map(
        local,
        mesh=mesh,
        in_specs=(rows, rows, rows, rows, rows, P(("groups", "tm"))),
        out_specs=(rows, rows, rows, rows),
        check_vma=False,
    )
```
